32 devices in a mesh: mode: 8 (over z, core), cols: 4 (over y, x).
Axes of the slice: x: 2, y: 2, z: 4, core: 2. Of those that a mesh axis runs over, the one named last changes fastest.
Arguments:
- snapshots: float32 [512, 32768], P('mode', 'cols'), may hold values from -54 to 54, as said below
- start_basis: float32 [512, 128], replicated, may hold values from -6 to 6
Outputs:
- subspace_basis: float32 [512, 128], replicated
- core_tensor: float32 [128, 32768], P('mode', 'cols')
The draws below stay inside these ranges and needn't reach their ends.
Inputs may be any that keep to these rules, and one draw needn't show every extreme that they name: `snapshots`: entries are finite real values.
All inputs are finite; a program needn't handle non-finite values.
Results may differ from the reference program's by a relative error of at most 0.00017.
Values sent between devices are 32-bit elements; how exact they have to be, the bound alone decides.
A program may use at most 64 MiB of HBM per device.

```python
import math
import jax
import jax.numpy as jnp
from jax import lax

I1 = 512
RANK = 128
COLS = 32768


def draw_snapshots(key, part):
    key_base = jax.random.fold_in(key, 11)
    key_rows = jax.random.fold_in(key, 12)
    key_cols = jax.random.fold_in(key, 13)
    base_field = jnp.clip(jax.random.normal(key_base, (I1, COLS), jnp.float32), -6.0, 6.0)
    row_scale = jnp.exp(jax.random.uniform(key_rows, (I1,), jnp.float32) * math.log(16.0)) / 16.0
    ramp = 1.0 + 2.0 * jnp.arange(COLS, dtype=jnp.float32) / COLS
    col_scale = jnp.exp(jax.random.uniform(key_cols, (COLS,), jnp.float32) * math.log(3.0)) * ramp
    return base_field * row_scale[:, None] * col_scale[None, :]


def gaussian(own_key, extent, deviation, bound, held_as=jnp.bfloat16):
    entries = jax.random.normal(own_key, extent, jnp.float32) * deviation
    return jnp.minimum(jnp.maximum(entries, -bound), bound).astype(held_as)


def setup_inputs(seed: int = 0) -> dict:
    streams_of = jax.random.split(jax.random.key(seed), 3)
    return {
        "snapshots": draw_snapshots(jax.random.fold_in(streams_of[2], 71), 0),
        "start_basis": gaussian(streams_of[1], (I1, RANK), 1.0, 6.0, jnp.float32),
    }


def orthonormal(projected):
    current = projected
    for sweep in range(2):
        inner = jnp.dot(current.T.astype(jnp.float32), current.astype(jnp.float32), precision=lax.Precision.HIGHEST, preferred_element_type=jnp.float32)
        lower_part = jnp.linalg.cholesky(inner)
        current = jax.scipy.linalg.solve_triangular(lower_part, current.T, lower=True).T
    return current

def reference(snapshots, start_basis):
    gram_full = jnp.dot(snapshots.astype(jnp.float32), snapshots.T.astype(jnp.float32), precision=lax.Precision.HIGHEST, preferred_element_type=jnp.float32)
    factor = jnp.linalg.cholesky(gram_full)
    inner_step = jnp.dot(factor.T.astype(jnp.float32), start_basis.astype(jnp.float32), precision=lax.Precision.HIGHEST, preferred_element_type=jnp.float32)
    projected = jnp.dot(factor.astype(jnp.float32), inner_step.astype(jnp.float32), precision=lax.Precision.HIGHEST, preferred_element_type=jnp.float32)
    subspace_basis = orthonormal(projected)
    core_tensor = jnp.dot(subspace_basis.T.astype(jnp.float32), snapshots.astype(jnp.float32), precision=lax.Precision.HIGHEST, preferred_element_type=jnp.float32)
    return (subspace_basis, core_tensor)
```

```python
import functools

import jax
import jax.numpy as jnp
from jax import lax
from jax.experimental import pallas as pl
from jax.experimental.pallas import tpu as pltpu
from jax.sharding import PartitionSpec as P

MESH = pl.DeviceIdType.MESH
SUB = 8


def dot(a, b, dims):
    return lax.dot_general(
        a,
        b,
        (dims, ((), ())),
        precision=lax.Precision.HIGHEST,
        preferred_element_type=jnp.float32,
    )


def greet(modes, cols):
    me, mc = lax.axis_index("mode"), lax.axis_index("cols")
    barrier = pltpu.get_barrier_semaphore()
    for d in range(1, modes):
        pl.semaphore_signal(
            barrier, inc=1, device_id={"mode": lax.rem(me + d, modes)}, device_id_type=MESH
        )
    for d in range(1, cols):
        pl.semaphore_signal(
            barrier, inc=1, device_id={"cols": lax.rem(mc + d, cols)}, device_id_type=MESH
        )
    pl.semaphore_wait(barrier, modes - 1 + cols - 1)


def gather_kernel(
    modes, cols, parts,
    x_ref, b_ref, f_ref, p_ref,
    part, piece, slots_c, slots_m,
    own_sem, s0, r0, s1, r1, s2, r2, s3, r3, s4, r4,
):
    me, mc = lax.axis_index("mode"), lax.axis_index("cols")
    rows = x_ref.shape[0]
    width = f_ref.shape[1]
    cw = width // parts
    whole = f_ref.shape[0]

    def put(src, dst, send, recv, axis, peer):
        return pltpu.make_async_remote_copy(
            src_ref=src, dst_ref=dst, send_sem=send, recv_sem=recv,
            device_id={axis: peer}, device_id_type=MESH,
        )

    my_rows = pl.ds(pl.multiple_of(me * rows, rows), rows)
    own = []
    for k in range(parts):
        copy = pltpu.make_async_copy(
            x_ref.at[:, pl.ds(pl.multiple_of(me * width + k * cw, cw), cw)],
            f_ref.at[my_rows, pl.ds(k * cw, cw)],
            own_sem.at[k],
        )
        copy.start()
        own.append(copy)

    greet(modes, cols)

    sent = []
    for k in range(parts):
        row = []
        for d in range(modes - 1, 0, -1):
            peer = lax.rem(me + d, modes)
            copy = put(
                x_ref.at[:, pl.ds(pl.multiple_of(peer * width + k * cw, cw), cw)],
                f_ref.at[my_rows, pl.ds(k * cw, cw)],
                s0.at[k * (modes - 1) + d - 1], r0.at[k * (modes - 1) + d - 1], "mode", peer,
            )
            copy.start()
            row.append(copy)
        sent.append(row)

    bt = b_ref[...].T
    for k in range(parts):
        own[k].wait()
        for copy in sent[k]:
            copy.wait_recv()
        fk = f_ref[:, pl.ds(k * cw, cw)]
        t = dot(bt, fk, ((1,), (0,)))
        term = dot(fk, t, ((1,), (1,)))
        if k == 0:
            part[...] = term
        else:
            part[...] += term

    rc = whole // cols
    mine = pl.ds(pl.multiple_of(mc * rc, rc), rc)
    first = []
    for d in range(1, cols):
        peer = lax.rem(mc + d, cols)
        copy = put(
            part.at[pl.ds(pl.multiple_of(peer * rc, rc), rc)],
            slots_c.at[d - 1], s1.at[d - 1], r1.at[d - 1], "cols", peer,
        )
        copy.start()
        first.append(copy)
    for copy in first:
        copy.wait_recv()
    total = part[mine, :]
    for d in range(1, cols):
        total = total + slots_c[d - 1]
    piece[...] = total

    sl = slots_m.shape[1]
    owners = rc // sl

    def guarded(flag, body):
        if owners == modes:
            body()
        else:
            pl.when(flag)(body)

    second = []
    for d in range(1, modes):
        peer = lax.rem(me + d, modes)
        place = peer if owners == modes else lax.rem(peer, owners)
        copy = put(
            piece.at[pl.ds(pl.multiple_of(place * sl, sl), sl)],
            slots_m.at[d - 1], s2.at[d - 1], r2.at[d - 1], "mode", peer,
        )
        guarded(peer < owners, copy.start)
        second.append((copy, peer))
    for copy, _ in second:
        guarded(me < owners, copy.wait_recv)
    place = me if owners == modes else lax.rem(me, owners)
    target = pl.ds(pl.multiple_of(mc * rc + place * sl, sl), sl)

    def add():
        total = piece[pl.ds(pl.multiple_of(place * sl, sl), sl), :]
        for d in range(1, modes):
            total = total + slots_m[d - 1]
        p_ref[target, :] = total

    guarded(me < owners, add)

    third = []
    for d in range(1, modes):
        peer = lax.rem(me + d, modes)
        copy = put(p_ref.at[target], p_ref.at[target], s3.at[d - 1], r3.at[d - 1], "mode", peer)
        guarded(me < owners, copy.start)
        third.append(copy)
    for d in range(1, modes):
        source = lax.rem(me + modes - d, modes)
        guarded(source < owners, third[d - 1].wait_recv)
    fourth = []
    for d in range(1, cols):
        peer = lax.rem(mc + d, cols)
        copy = put(p_ref.at[mine], p_ref.at[mine], s4.at[d - 1], r4.at[d - 1], "cols", peer)
        copy.start()
        fourth.append(copy)
    for copy in fourth:
        copy.wait_recv()

    for row in sent:
        for copy in row:
            copy.wait_send()
    for copy in first:
        copy.wait_send()
    for copy, peer in second:
        guarded(peer < owners, copy.wait_send)
    for copy in third:
        guarded(me < owners, copy.wait_send)
    for copy in fourth:
        copy.wait_send()


def gather(modes, cols, x, b):
    rows, local = x.shape
    whole, width = rows * modes, local // modes
    rank = b.shape[1]
    parts = 2 if width % 256 == 0 else 1
    rc = whole // cols
    sl = max(SUB, rc // modes)
    dma = pltpu.SemaphoreType.DMA
    vmem = pl.BlockSpec(memory_space=pltpu.VMEM)
    return pl.pallas_call(
        functools.partial(gather_kernel, modes, cols, parts),
        out_shape=(
            jax.ShapeDtypeStruct((whole, width), jnp.float32),
            jax.ShapeDtypeStruct((whole, rank), jnp.float32),
        ),
        in_specs=[pl.BlockSpec(memory_space=pl.ANY), vmem],
        out_specs=(vmem, vmem),
        scratch_shapes=[
            pltpu.VMEM((whole, rank), jnp.float32),
            pltpu.VMEM((rc, rank), jnp.float32),
            pltpu.VMEM((cols - 1, rc, rank), jnp.float32),
            pltpu.VMEM((modes - 1, sl, rank), jnp.float32),
            dma((parts,)),
            dma((parts * (modes - 1),)), dma((parts * (modes - 1),)),
            dma((cols - 1,)), dma((cols - 1,)),
            dma((modes - 1,)), dma((modes - 1,)),
            dma((modes - 1,)), dma((modes - 1,)),
            dma((cols - 1,)), dma((cols - 1,)),
        ],
        compiler_params=pltpu.CompilerParams(
            collective_id=0, has_side_effects=True, vmem_limit_bytes=32 * 2**20
        ),
        name="gather_project",
    )(x, b)


def inverse_factor(a, out_ref):
    n = a.shape[0]
    count = n // SUB
    shape = (SUB, n)
    row_id = lax.broadcasted_iota(jnp.int32, shape, 0)
    col_id = lax.broadcasted_iota(jnp.int32, shape, 1)
    blocks = [a[SUB * i:SUB * (i + 1), :] for i in range(count)]
    duals = [
        jnp.where(col_id == row_id + SUB * i, 1.0, 0.0).astype(jnp.float32) for i in range(count)
    ]
    for j in range(0, n, 2):
        at, jj = j // SUB, j % SUB
        block, dual = blocks[at], duals[at]
        u0, u1 = (jnp.broadcast_to(block[jj + i:jj + i + 1, :], shape) for i in range(2))
        v0, v1 = (jnp.broadcast_to(dual[jj + i:jj + i + 1, :], shape) for i in range(2))
        p = jnp.broadcast_to(u0[:, j:j + 1], shape)
        q = jnp.broadcast_to(u0[:, j + 1:j + 2], shape)
        r = jnp.broadcast_to(u1[:, j + 1:j + 2], shape)
        idet = 1.0 / (p * r - q * q)
        i00, i01, i11 = r * idet, -q * idet, p * idet
        x0, x1 = i00 * u0 + i01 * u1, i01 * u0 + i11 * u1
        y0, y1 = i00 * v0 + i01 * v1, i01 * v0 + i11 * v1
        out_ref[j:j + 1, :] = (v0 * lax.rsqrt(p))[0:1, :]
        out_ref[j + 1:j + 2, :] = ((v1 - (q / p) * v0) * jnp.sqrt(i11))[0:1, :]
        for i in range(at, count):
            c0 = jnp.broadcast_to(blocks[i][:, j:j + 1], shape)
            c1 = jnp.broadcast_to(blocks[i][:, j + 1:j + 2], shape)
            if i == at:
                if jj + 2 == SUB:
                    continue
                later = row_id > jj + 1
                c0, c1 = jnp.where(later, c0, 0.0), jnp.where(later, c1, 0.0)
            blocks[i] = blocks[i] - (c0 * x0 + c1 * x1)
            duals[i] = duals[i] - (c0 * y0 + c1 * y1)


def basis_kernel(p_ref, u_ref, inverse):
    rank = p_ref.shape[1]
    rows = lax.broadcasted_iota(jnp.int32, (rank, rank), 0)
    columns = lax.broadcasted_iota(jnp.int32, (rank, rank), 1)
    eye = jnp.where(rows == columns, 1.0, 0.0).astype(jnp.float32)
    half = jnp.where(rows > columns, 1.0, 0.5 * eye)

    p = p_ref[...]
    p = p * lax.rsqrt(jnp.sum(p * p, axis=0, keepdims=True))
    inverse_factor(dot(p, p, ((0,), (0,))), inverse)
    q = dot(p, inverse[...], ((1,), (1,)))

    a = dot(q, q, ((0,), (0,)))
    e = a - eye
    near = jnp.sum(e * e) < 1e-4

    @pl.when(near)
    def _():
        x = eye - half * e
        e1 = dot(dot(x, a, ((1,), (0,))), x, ((1,), (1,))) - eye
        inverse[...] = x - dot(half * e1, x, ((1,), (0,)))

    @pl.when(jnp.logical_not(near))
    def _():
        inverse_factor(a, inverse)

    u_ref[...] = dot(q, inverse[...], ((1,), (1,)))


def basis(p):
    vmem = pl.BlockSpec(memory_space=pltpu.VMEM)
    rank = p.shape[1]
    return pl.pallas_call(
        basis_kernel,
        out_shape=jax.ShapeDtypeStruct(p.shape, jnp.float32),
        in_specs=[vmem],
        out_specs=vmem,
        scratch_shapes=[pltpu.VMEM((rank, rank), jnp.float32)],
        compiler_params=pltpu.CompilerParams(vmem_limit_bytes=32 * 2**20),
        name="orthonormal_basis",
    )(p)


def core_kernel(modes, parts, u_ref, f_ref, c_ref, local, send, recv, own_sem):
    me = lax.axis_index("mode")
    greet(modes, 1)
    width = f_ref.shape[1]
    cw = width // parts
    rows = c_ref.shape[0]
    ut = u_ref[...].T
    sent = []
    for k in range(parts):
        local[:, pl.ds(k * cw, cw)] = dot(ut, f_ref[:, pl.ds(k * cw, cw)], ((1,), (0,)))
        here = pl.ds(pl.multiple_of(me * width + k * cw, cw), cw)
        for d in range(modes - 1, 0, -1):
            peer = lax.rem(me + d, modes)
            copy = pltpu.make_async_remote_copy(
                src_ref=local.at[pl.ds(pl.multiple_of(peer * rows, rows), rows), pl.ds(k * cw, cw)],
                dst_ref=c_ref.at[:, here],
                send_sem=send.at[k * (modes - 1) + d - 1],
                recv_sem=recv.at[k * (modes - 1) + d - 1],
                device_id={"mode": peer}, device_id_type=MESH,
            )
            copy.start()
            sent.append(copy)
    own = pltpu.make_async_copy(
        local.at[pl.ds(pl.multiple_of(me * rows, rows), rows)],
        c_ref.at[:, pl.ds(pl.multiple_of(me * width, width), width)],
        own_sem,
    )
    own.start()
    own.wait()
    for copy in sent:
        copy.wait()


def core(modes, u, f):
    whole, width = f.shape
    rank = u.shape[1]
    parts = 2 if width % 256 == 0 else 1
    vmem = pl.BlockSpec(memory_space=pltpu.VMEM)
    dma = pltpu.SemaphoreType.DMA
    return pl.pallas_call(
        functools.partial(core_kernel, modes, parts),
        out_shape=jax.ShapeDtypeStruct((rank // modes, width * modes), jnp.float32),
        in_specs=[vmem, vmem],
        out_specs=vmem,
        scratch_shapes=[
            pltpu.VMEM((rank, width), jnp.float32),
            dma((parts * (modes - 1),)), dma((parts * (modes - 1),)),
            dma,
        ],
        compiler_params=pltpu.CompilerParams(
            collective_id=1, has_side_effects=True, vmem_limit_bytes=32 * 2**20
        ),
        name="core_tensor",
    )(u, f)


def solution(mesh):
    modes, cols = mesh.shape["mode"], mesh.shape["cols"]

    def shards(snapshots, start_basis):
        fibres, projected = gather(modes, cols, snapshots, start_basis)
        subspace_basis = basis(projected)
        return subspace_basis, core(modes, subspace_basis, fibres)

    return jax.shard_map(
        shards,
        mesh=mesh,
        in_specs=(P("mode", "cols"), P()),
        out_specs=(P(), P("mode", "cols")),
        check_vma=False,
    )
```

```python
import functools

import jax
import jax.numpy as jnp
from jax import lax
from jax.experimental import pallas as pl
from jax.experimental.pallas import tpu as pltpu
from jax.sharding import PartitionSpec as P

MESH = pl.DeviceIdType.MESH
SUB = 8


def dot(a, b, dims):
    return lax.dot_general(
        a,
        b,
        (dims, ((), ())),
        precision=lax.Precision.HIGHEST,
        preferred_element_type=jnp.float32,
    )


def pairing(me, d, modes):
    if modes & (modes - 1):
        return lax.rem(me + d, modes)
    peer = me
    bit = 1
    while bit < modes:
        if d & bit:
            peer = peer + bit * (1 - 2 * lax.rem(me // bit, 2))
        bit *= 2
    return peer


def small(a, b, dims):
    return lax.dot_general(a, b, (dims, ((), ())), preferred_element_type=jnp.float32)


def greet(modes, cols):
    me, mc = lax.axis_index("mode"), lax.axis_index("cols")
    barrier = pltpu.get_barrier_semaphore()
    for d in range(1, modes):
        pl.semaphore_signal(
            barrier, inc=1, device_id={"mode": lax.rem(me + d, modes)}, device_id_type=MESH
        )
    for d in range(1, cols):
        pl.semaphore_signal(
            barrier, inc=1, device_id={"cols": lax.rem(mc + d, cols)}, device_id_type=MESH
        )
    return lambda: pl.semaphore_wait(barrier, modes - 1 + cols - 1)


def gather_kernel(
    modes, cols, parts,
    x_ref, b_ref, f_ref, p_ref,
    basis, part, piece, slots_c, slots_m,
    own_sem, basis_sem, s0, r0, s1, r1, s2, r2, s3, r3, s4, r4,
):
    me, mc = lax.axis_index("mode"), lax.axis_index("cols")
    rows = x_ref.shape[0]
    width = f_ref.shape[1]
    cw = width // parts
    whole = f_ref.shape[0]

    def put(src, dst, send, recv, axis, peer):
        return pltpu.make_async_remote_copy(
            src_ref=src, dst_ref=dst, send_sem=send, recv_sem=recv,
            device_id={axis: peer}, device_id_type=MESH,
        )

    my_rows = pl.ds(pl.multiple_of(me * rows, rows), rows)
    everyone = greet(modes, cols)
    start = pltpu.make_async_copy(b_ref, basis, basis_sem)
    start.start()
    own = []
    for k in range(parts):
        copy = pltpu.make_async_copy(
            x_ref.at[:, pl.ds(pl.multiple_of(me * width + k * cw, cw), cw)],
            f_ref.at[my_rows, pl.ds(k * cw, cw)],
            own_sem.at[k],
        )
        copy.start()
        own.append(copy)

    everyone()

    sent = [[] for _ in range(parts)]

    def send(k, rounds):
        for d in rounds:
            peer = pairing(me, d, modes)
            copy = put(
                x_ref.at[:, pl.ds(pl.multiple_of(peer * width + k * cw, cw), cw)],
                f_ref.at[my_rows, pl.ds(k * cw, cw)],
                s0.at[k * (modes - 1) + d - 1], r0.at[k * (modes - 1) + d - 1], "mode", peer,
            )
            copy.start()
            sent[k].append(copy)

    far = range(modes - 1, modes // 2 - 1, -1)
    near = range(modes // 2 - 1, 0, -1)
    for k in range(parts):
        send(k, far)
        if k > 0:
            send(k - 1, near)
    send(parts - 1, near)

    start.wait()
    bt = basis[...].T
    for k in range(parts):
        own[k].wait()
        for copy in sent[k]:
            copy.wait_recv()
        fk = f_ref[:, pl.ds(k * cw, cw)]
        t = dot(bt, fk, ((1,), (0,)))
        term = dot(fk, t, ((1,), (1,)))
        if k == 0:
            part[...] = term
        else:
            part[...] += term

    rc = whole // cols
    mine = pl.ds(pl.multiple_of(mc * rc, rc), rc)
    first = []
    for d in range(1, cols):
        peer = lax.rem(mc + d, cols)
        copy = put(
            part.at[pl.ds(pl.multiple_of(peer * rc, rc), rc)],
            slots_c.at[d - 1], s1.at[d - 1], r1.at[d - 1], "cols", peer,
        )
        copy.start()
        first.append(copy)
    for copy in first:
        copy.wait_recv()
    total = part[mine, :]
    for d in range(1, cols):
        total = total + slots_c[d - 1]
    piece[...] = total

    sl = slots_m.shape[1]
    owners = rc // sl

    def guarded(flag, body):
        if owners == modes:
            body()
        else:
            pl.when(flag)(body)

    second = []
    for d in range(modes - 1, 0, -1):
        peer = pairing(me, d, modes)
        place = peer if owners == modes else lax.rem(peer, owners)
        copy = put(
            piece.at[pl.ds(pl.multiple_of(place * sl, sl), sl)],
            slots_m.at[d - 1], s2.at[d - 1], r2.at[d - 1], "mode", peer,
        )
        guarded(peer < owners, copy.start)
        second.append((copy, peer))
    for copy, _ in second:
        guarded(me < owners, copy.wait_recv)
    place = me if owners == modes else lax.rem(me, owners)
    target = pl.ds(pl.multiple_of(mc * rc + place * sl, sl), sl)

    def add():
        total = piece[pl.ds(pl.multiple_of(place * sl, sl), sl), :]
        for d in range(1, modes):
            total = total + slots_m[d - 1]
        p_ref[target, :] = total

    guarded(me < owners, add)

    third = []
    for d in range(modes - 1, 0, -1):
        peer = pairing(me, d, modes)
        copy = put(p_ref.at[target], p_ref.at[target], s3.at[d - 1], r3.at[d - 1], "mode", peer)
        guarded(me < owners, copy.start)
        third.append(copy)
    fourth = []

    def forward(d, source):
        spot = source if owners == modes else lax.rem(source, owners)
        rows_of = pl.ds(pl.multiple_of(mc * rc + spot * sl, sl), sl)
        for e in range(1, cols):
            at = d * (cols - 1) + e - 1
            copy = put(
                p_ref.at[rows_of], p_ref.at[rows_of], s4.at[at], r4.at[at],
                "cols", lax.rem(mc + e, cols),
            )
            guarded(source < owners, copy.start)
            fourth.append((copy, source))

    forward(0, me)
    for d in range(1, modes):
        source = pairing(me, d, modes) if modes & (modes - 1) == 0 else lax.rem(me + modes - d, modes)
        guarded(source < owners, third[modes - 1 - d].wait_recv)
        forward(d, source)
    for copy, source in fourth:
        guarded(source < owners, copy.wait_recv)

    for row in sent:
        for copy in row:
            copy.wait_send()
    for copy in first:
        copy.wait_send()
    for copy, peer in second:
        guarded(peer < owners, copy.wait_send)
    for copy in third:
        guarded(me < owners, copy.wait_send)
    for copy, source in fourth:
        guarded(source < owners, copy.wait_send)


def gather(modes, cols, x, b):
    rows, local = x.shape
    whole, width = rows * modes, local // modes
    rank = b.shape[1]
    parts = 4 if width % 512 == 0 else 1
    rc = whole // cols
    sl = max(SUB, rc // modes)
    dma = pltpu.SemaphoreType.DMA
    vmem = pl.BlockSpec(memory_space=pltpu.VMEM)
    return pl.pallas_call(
        functools.partial(gather_kernel, modes, cols, parts),
        out_shape=(
            jax.ShapeDtypeStruct((whole, width), jnp.float32),
            jax.ShapeDtypeStruct((whole, rank), jnp.float32),
        ),
        in_specs=[pl.BlockSpec(memory_space=pltpu.HBM)] * 2,
        out_specs=(vmem, vmem),
        scratch_shapes=[
            pltpu.VMEM((whole, rank), jnp.float32),
            pltpu.VMEM((whole, rank), jnp.float32),
            pltpu.VMEM((rc, rank), jnp.float32),
            pltpu.VMEM((cols - 1, rc, rank), jnp.float32),
            pltpu.VMEM((modes - 1, sl, rank), jnp.float32),
            dma((parts,)), dma,
            dma((parts * (modes - 1),)), dma((parts * (modes - 1),)),
            dma((cols - 1,)), dma((cols - 1,)),
            dma((modes - 1,)), dma((modes - 1,)),
            dma((modes - 1,)), dma((modes - 1,)),
            dma((modes * (cols - 1),)), dma((modes * (cols - 1),)),
        ],
        compiler_params=pltpu.CompilerParams(
            collective_id=0, has_side_effects=True, vmem_limit_bytes=32 * 2**20
        ),
        name="gather_project",
    )(x, b)


def inverse_factor(a, out_ref):
    n = a.shape[0]
    count = n // SUB
    shape = (SUB, n)
    row_id = lax.broadcasted_iota(jnp.int32, shape, 0)
    col_id = lax.broadcasted_iota(jnp.int32, shape, 1)
    blocks = [a[SUB * i:SUB * (i + 1), :] for i in range(count)]
    duals = [
        jnp.where(col_id == row_id + SUB * i, 1.0, 0.0).astype(jnp.float32) for i in range(count)
    ]
    for j in range(0, n, 2):
        at, jj = j // SUB, j % SUB
        block, dual = blocks[at], duals[at]
        u0, u1 = (jnp.broadcast_to(block[jj + i:jj + i + 1, :], shape) for i in range(2))
        v0, v1 = (jnp.broadcast_to(dual[jj + i:jj + i + 1, :], shape) for i in range(2))
        p = jnp.broadcast_to(u0[:, j:j + 1], shape)
        q = jnp.broadcast_to(u0[:, j + 1:j + 2], shape)
        r = jnp.broadcast_to(u1[:, j + 1:j + 2], shape)
        idet = 1.0 / (p * r - q * q)
        i00, i01, i11 = r * idet, -q * idet, p * idet
        x0, x1 = i00 * u0 + i01 * u1, i01 * u0 + i11 * u1
        y0, y1 = i00 * v0 + i01 * v1, i01 * v0 + i11 * v1
        out_ref[j:j + 1, :] = (v0 * lax.rsqrt(p))[0:1, :]
        out_ref[j + 1:j + 2, :] = ((v1 - (q / p) * v0) * jnp.sqrt(i11))[0:1, :]
        for i in range(at, count):
            c0 = jnp.broadcast_to(blocks[i][:, j:j + 1], shape)
            c1 = jnp.broadcast_to(blocks[i][:, j + 1:j + 2], shape)
            if i == at:
                if jj + 2 == SUB:
                    continue
                later = row_id > jj + 1
                c0, c1 = jnp.where(later, c0, 0.0), jnp.where(later, c1, 0.0)
            blocks[i] = blocks[i] - (c0 * x0 + c1 * x1)
            duals[i] = duals[i] - (c0 * y0 + c1 * y1)


def basis_kernel(p_ref, u_ref, ut_ref, inverse):
    rank = p_ref.shape[1]
    rows = lax.broadcasted_iota(jnp.int32, (rank, rank), 0)
    columns = lax.broadcasted_iota(jnp.int32, (rank, rank), 1)
    eye = jnp.where(rows == columns, 1.0, 0.0).astype(jnp.float32)
    half = jnp.where(rows > columns, 1.0, 0.5 * eye)

    p = p_ref[...]
    p = p * lax.rsqrt(jnp.sum(p * p, axis=0, keepdims=True))
    inverse_factor(dot(p, p, ((0,), (0,))), inverse)
    q = dot(p, inverse[...], ((1,), (1,)))

    a = dot(q, q, ((0,), (0,)))
    e = a - eye
    near = jnp.sum(e * e) < 1e-6

    @pl.when(near)
    def _():
        low = half * e
        m = small(low, e, ((1,), (0,)))
        e1 = small(low + m, low, ((1,), (1,))) - m - m.T
        low1 = half * e1
        step = low + low1 - small(low1, low, ((1,), (0,)))
        u_ref[...] = q - small(q, step, ((1,), (1,)))

    @pl.when(jnp.logical_not(near))
    def _():
        inverse_factor(a, inverse)
        u_ref[...] = dot(q, inverse[...], ((1,), (1,)))

    ut_ref[...] = u_ref[...].T


def basis(p):
    vmem = pl.BlockSpec(memory_space=pltpu.VMEM)
    rank = p.shape[1]
    return pl.pallas_call(
        basis_kernel,
        out_shape=(
            jax.ShapeDtypeStruct(p.shape, jnp.float32),
            jax.ShapeDtypeStruct((rank, p.shape[0]), jnp.float32),
        ),
        in_specs=[vmem],
        out_specs=(vmem, vmem),
        scratch_shapes=[pltpu.VMEM((rank, rank), jnp.float32)],
        compiler_params=pltpu.CompilerParams(vmem_limit_bytes=32 * 2**20),
        name="orthonormal_basis",
    )(p)


def core_kernel(modes, parts, ut_ref, f_ref, c_ref, local, send, recv, own_sem):
    me = lax.axis_index("mode")
    everyone = greet(modes, 1)
    width = f_ref.shape[1]
    cw = width // parts
    rows = c_ref.shape[0]
    sent = []
    for k in range(parts):
        local[:, pl.ds(k * cw, cw)] = dot(ut_ref[...], f_ref[:, pl.ds(k * cw, cw)], ((1,), (0,)))
        if k == 0:
            everyone()
        here = pl.ds(pl.multiple_of(me * width + k * cw, cw), cw)
        for d in range(modes - 1, 0, -1):
            peer = pairing(me, d, modes)
            copy = pltpu.make_async_remote_copy(
                src_ref=local.at[pl.ds(pl.multiple_of(peer * rows, rows), rows), pl.ds(k * cw, cw)],
                dst_ref=c_ref.at[:, here],
                send_sem=send.at[k * (modes - 1) + d - 1],
                recv_sem=recv.at[k * (modes - 1) + d - 1],
                device_id={"mode": peer}, device_id_type=MESH,
            )
            copy.start()
            sent.append(copy)
    own = pltpu.make_async_copy(
        local.at[pl.ds(pl.multiple_of(me * rows, rows), rows)],
        c_ref.at[:, pl.ds(pl.multiple_of(me * width, width), width)],
        own_sem,
    )
    own.start()
    own.wait()
    for copy in sent:
        copy.wait()


def core(modes, ut, f):
    whole, width = f.shape
    rank = ut.shape[0]
    parts = 4 if width % 512 == 0 else 1
    vmem = pl.BlockSpec(memory_space=pltpu.VMEM)
    dma = pltpu.SemaphoreType.DMA
    return pl.pallas_call(
        functools.partial(core_kernel, modes, parts),
        out_shape=jax.ShapeDtypeStruct((rank // modes, width * modes), jnp.float32),
        in_specs=[vmem, vmem],
        out_specs=vmem,
        scratch_shapes=[
            pltpu.VMEM((rank, width), jnp.float32),
            dma((parts * (modes - 1),)), dma((parts * (modes - 1),)),
            dma,
        ],
        compiler_params=pltpu.CompilerParams(
            collective_id=1, has_side_effects=True, vmem_limit_bytes=32 * 2**20
        ),
        name="core_tensor",
    )(ut, f)


def solution(mesh):
    modes, cols = mesh.shape["mode"], mesh.shape["cols"]

    def shards(snapshots, start_basis):
        fibres, projected = gather(modes, cols, snapshots, start_basis)
        subspace_basis, transposed = basis(projected)
        return subspace_basis, core(modes, transposed, fibres)

    return jax.shard_map(
        shards,
        mesh=mesh,
        in_specs=(P("mode", "cols"), P()),
        out_specs=(P(), P("mode", "cols")),
        check_vma=False,
    )
```

```python
import functools

import jax
import jax.numpy as jnp
from jax import lax
from jax.experimental import pallas as pl
from jax.experimental.pallas import tpu as pltpu
from jax.sharding import PartitionSpec as P

MESH = pl.DeviceIdType.MESH
SUB = 8


def dot(a, b, dims):
    return lax.dot_general(
        a,
        b,
        (dims, ((), ())),
        precision=lax.Precision.HIGHEST,
        preferred_element_type=jnp.float32,
    )


def pairing(me, d, modes):
    if modes & (modes - 1):
        return lax.rem(me + d, modes)
    peer = me
    bit = 1
    while bit < modes:
        if d & bit:
            peer = peer + bit * (1 - 2 * lax.rem(me // bit, 2))
        bit *= 2
    return peer


def small(a, b, dims):
    return lax.dot_general(a, b, (dims, ((), ())), preferred_element_type=jnp.float32)


def greet(modes, cols):
    me, mc = lax.axis_index("mode"), lax.axis_index("cols")
    barrier = pltpu.get_barrier_semaphore()
    for d in range(1, modes):
        pl.semaphore_signal(
            barrier, inc=1, device_id={"mode": lax.rem(me + d, modes)}, device_id_type=MESH
        )
    for d in range(1, cols):
        pl.semaphore_signal(
            barrier, inc=1, device_id={"cols": lax.rem(mc + d, cols)}, device_id_type=MESH
        )
    return lambda: pl.semaphore_wait(barrier, modes - 1 + cols - 1)


def gather_kernel(
    modes, cols, parts,
    x_ref, b_ref, f_ref, p_ref,
    basis, part, piece, slots_c, slots_m,
    own_sem, basis_sem, s0, r0, s1, r1, s2, r2, s3, r3, s4, r4,
):
    me, mc = lax.axis_index("mode"), lax.axis_index("cols")
    rows = x_ref.shape[0]
    width = f_ref.shape[1]
    cw = width // parts
    whole = f_ref.shape[0]

    def put(src, dst, send, recv, axis, peer):
        return pltpu.make_async_remote_copy(
            src_ref=src, dst_ref=dst, send_sem=send, recv_sem=recv,
            device_id={axis: peer}, device_id_type=MESH,
        )

    my_rows = pl.ds(pl.multiple_of(me * rows, rows), rows)
    everyone = greet(modes, cols)
    start = pltpu.make_async_copy(b_ref, basis, basis_sem)
    start.start()
    own = []
    for k in range(parts):
        copy = pltpu.make_async_copy(
            x_ref.at[:, pl.ds(pl.multiple_of(me * width + k * cw, cw), cw)],
            f_ref.at[my_rows, pl.ds(k * cw, cw)],
            own_sem.at[k],
        )
        copy.start()
        own.append(copy)

    everyone()

    sent = [[] for _ in range(parts)]

    def send(k, rounds):
        for d in rounds:
            peer = pairing(me, d, modes)
            copy = put(
                x_ref.at[:, pl.ds(pl.multiple_of(peer * width + k * cw, cw), cw)],
                f_ref.at[my_rows, pl.ds(k * cw, cw)],
                s0.at[k * (modes - 1) + d - 1], r0.at[k * (modes - 1) + d - 1], "mode", peer,
            )
            copy.start()
            sent[k].append(copy)

    far = range(modes - 1, modes // 2 - 1, -1)
    near = range(modes // 2 - 1, 0, -1)
    for k in range(parts):
        send(k, far)
        if k > 0:
            send(k - 1, near)
    send(parts - 1, near)

    start.wait()
    bt = basis[...].T
    for k in range(parts):
        own[k].wait()
        for copy in sent[k]:
            copy.wait_recv()
        fk = f_ref[:, pl.ds(k * cw, cw)]
        t = dot(bt, fk, ((1,), (0,)))
        term = dot(fk, t, ((1,), (1,)))
        if k == 0:
            part[...] = term
        else:
            part[...] += term

    rc = whole // cols
    mine = pl.ds(pl.multiple_of(mc * rc, rc), rc)
    first = []
    for d in range(1, cols):
        peer = lax.rem(mc + d, cols)
        copy = put(
            part.at[pl.ds(pl.multiple_of(peer * rc, rc), rc)],
            slots_c.at[d - 1], s1.at[d - 1], r1.at[d - 1], "cols", peer,
        )
        copy.start()
        first.append(copy)
    for copy in first:
        copy.wait_recv()
    total = part[mine, :]
    for d in range(1, cols):
        total = total + slots_c[d - 1]
    piece[...] = total

    sl = slots_m.shape[1]
    owners = rc // sl

    def guarded(flag, body):
        if owners == modes:
            body()
        else:
            pl.when(flag)(body)

    second = []
    for d in range(modes - 1, 0, -1):
        peer = pairing(me, d, modes)
        place = peer if owners == modes else lax.rem(peer, owners)
        copy = put(
            piece.at[pl.ds(pl.multiple_of(place * sl, sl), sl)],
            slots_m.at[d - 1], s2.at[d - 1], r2.at[d - 1], "mode", peer,
        )
        guarded(peer < owners, copy.start)
        second.append((copy, peer))
    for copy, _ in second:
        guarded(me < owners, copy.wait_recv)
    place = me if owners == modes else lax.rem(me, owners)
    target = pl.ds(pl.multiple_of(mc * rc + place * sl, sl), sl)

    def add():
        total = piece[pl.ds(pl.multiple_of(place * sl, sl), sl), :]
        for d in range(1, modes):
            total = total + slots_m[d - 1]
        p_ref[target, :] = total

    guarded(me < owners, add)

    third = []
    for d in range(modes - 1, 0, -1):
        peer = pairing(me, d, modes)
        copy = put(p_ref.at[target], p_ref.at[target], s3.at[d - 1], r3.at[d - 1], "mode", peer)
        guarded(me < owners, copy.start)
        third.append(copy)
    fourth = []

    def forward(d, source):
        spot = source if owners == modes else lax.rem(source, owners)
        rows_of = pl.ds(pl.multiple_of(mc * rc + spot * sl, sl), sl)
        for e in range(1, cols):
            at = d * (cols - 1) + e - 1
            copy = put(
                p_ref.at[rows_of], p_ref.at[rows_of], s4.at[at], r4.at[at],
                "cols", lax.rem(mc + e, cols),
            )
            guarded(source < owners, copy.start)
            fourth.append((copy, source))

    forward(0, me)
    for d in range(1, modes):
        source = pairing(me, d, modes) if modes & (modes - 1) == 0 else lax.rem(me + modes - d, modes)
        guarded(source < owners, third[modes - 1 - d].wait_recv)
        forward(d, source)
    for copy, source in fourth:
        guarded(source < owners, copy.wait_recv)

    for row in sent:
        for copy in row:
            copy.wait_send()
    for copy in first:
        copy.wait_send()
    for copy, peer in second:
        guarded(peer < owners, copy.wait_send)
    for copy in third:
        guarded(me < owners, copy.wait_send)
    for copy, source in fourth:
        guarded(source < owners, copy.wait_send)


def gather(modes, cols, x, b):
    rows, local = x.shape
    whole, width = rows * modes, local // modes
    rank = b.shape[1]
    parts = 4 if width % 512 == 0 else 1
    rc = whole // cols
    sl = max(SUB, rc // modes)
    dma = pltpu.SemaphoreType.DMA
    vmem = pl.BlockSpec(memory_space=pltpu.VMEM)
    return pl.pallas_call(
        functools.partial(gather_kernel, modes, cols, parts),
        out_shape=(
            jax.ShapeDtypeStruct((whole, width), jnp.float32),
            jax.ShapeDtypeStruct((whole, rank), jnp.float32),
        ),
        in_specs=[pl.BlockSpec(memory_space=pltpu.HBM)] * 2,
        out_specs=(vmem, vmem),
        scratch_shapes=[
            pltpu.VMEM((whole, rank), jnp.float32),
            pltpu.VMEM((whole, rank), jnp.float32),
            pltpu.VMEM((rc, rank), jnp.float32),
            pltpu.VMEM((cols - 1, rc, rank), jnp.float32),
            pltpu.VMEM((modes - 1, sl, rank), jnp.float32),
            dma((parts,)), dma,
            dma((parts * (modes - 1),)), dma((parts * (modes - 1),)),
            dma((cols - 1,)), dma((cols - 1,)),
            dma((modes - 1,)), dma((modes - 1,)),
            dma((modes - 1,)), dma((modes - 1,)),
            dma((modes * (cols - 1),)), dma((modes * (cols - 1),)),
        ],
        compiler_params=pltpu.CompilerParams(
            collective_id=0, has_side_effects=True, vmem_limit_bytes=32 * 2**20
        ),
        name="gather_project",
    )(x, b)


def tree(terms):
    while len(terms) > 1:
        terms = [sum(terms[i:i + 2][1:], terms[i]) for i in range(0, len(terms), 2)]
    return terms[0]


def inverse_factor(a, out_ref):
    n = a.shape[0]
    count = n // SUB
    shape = (SUB, n)
    row_id = lax.broadcasted_iota(jnp.int32, shape, 0)
    col_id = lax.broadcasted_iota(jnp.int32, shape, 1)
    blocks = [a[SUB * i:SUB * (i + 1), :] for i in range(count)]
    duals = [
        jnp.where(col_id == row_id + SUB * i, 1.0, 0.0).astype(jnp.float32) for i in range(count)
    ]

    def row(block, i):
        return jnp.broadcast_to(block[i:i + 1, :], shape)

    def column(block, j):
        return jnp.broadcast_to(block[:, j:j + 1], shape)

    for at in range(count):
        base = SUB * at
        diagonal = [column(blocks[at], base + k) for k in range(SUB)]
        block, dual, lower = blocks[at], duals[at], duals[at]
        for k in range(0, SUB, 2):
            c0, c1 = diagonal[k], diagonal[k + 1]
            p, q, r = row(c0, k), row(c1, k), row(c1, k + 1)
            idet = 1.0 / (p * r - q * q)
            i00, i01, i11 = r * idet, -q * idet, p * idet

            def solve(m):
                m0, m1 = row(m, k), row(m, k + 1)
                return i00 * m0 + i01 * m1, i01 * m0 + i11 * m1

            def step(m):
                x0, x1 = solve(m)
                rest = m - (c0 * x0 + c1 * x1)
                return jnp.where(row_id == k, x0, jnp.where(row_id == k + 1, x1, rest))

            for later in range(k + 2, SUB):
                diagonal[later] = step(diagonal[later])
            v0, v1 = row(lower, k), row(lower, k + 1)
            out_ref[base + k:base + k + 1, :] = (v0 * lax.rsqrt(p))[0:1, :]
            out_ref[base + k + 1:base + k + 2, :] = ((v1 - (q / p) * v0) * jnp.sqrt(i11))[0:1, :]
            if k + 2 < SUB:
                y0, y1 = solve(lower)
                lower = jnp.where(row_id > k + 1, lower - (c0 * y0 + c1 * y1), lower)
            block, dual = step(block), step(dual)
        if at + 1 == count:
            break
        xs = [row(block, k) for k in range(SUB)]
        ys = [row(dual, k) for k in range(SUB)]
        for i in range(at + 1, count):
            cs = [column(blocks[i], base + k) for k in range(SUB)]
            blocks[i] = blocks[i] - tree([c * x for c, x in zip(cs, xs)])
            duals[i] = duals[i] - tree([c * y for c, y in zip(cs, ys)])


def basis_kernel(p_ref, u_ref, ut_ref, inverse):
    rank = p_ref.shape[1]
    rows = lax.broadcasted_iota(jnp.int32, (rank, rank), 0)
    columns = lax.broadcasted_iota(jnp.int32, (rank, rank), 1)
    eye = jnp.where(rows == columns, 1.0, 0.0).astype(jnp.float32)
    half = jnp.where(rows > columns, 1.0, 0.5 * eye)

    p = p_ref[...]
    p = p * lax.rsqrt(jnp.sum(p * p, axis=0, keepdims=True))
    inverse_factor(dot(p, p, ((0,), (0,))), inverse)
    q = dot(p, inverse[...], ((1,), (1,)))

    a = dot(q, q, ((0,), (0,)))
    e = a - eye
    near = jnp.sum(e * e) < 1e-6

    @pl.when(near)
    def _():
        low = half * e
        m = small(low, e, ((1,), (0,)))
        e1 = small(low + m, low, ((1,), (1,))) - m - m.T
        low1 = half * e1
        step = low + low1 - small(low1, low, ((1,), (0,)))
        u_ref[...] = q - small(q, step, ((1,), (1,)))

    @pl.when(jnp.logical_not(near))
    def _():
        inverse_factor(a, inverse)
        u_ref[...] = dot(q, inverse[...], ((1,), (1,)))

    ut_ref[...] = u_ref[...].T


def basis(p):
    vmem = pl.BlockSpec(memory_space=pltpu.VMEM)
    rank = p.shape[1]
    return pl.pallas_call(
        basis_kernel,
        out_shape=(
            jax.ShapeDtypeStruct(p.shape, jnp.float32),
            jax.ShapeDtypeStruct((rank, p.shape[0]), jnp.float32),
        ),
        in_specs=[vmem],
        out_specs=(vmem, vmem),
        scratch_shapes=[pltpu.VMEM((rank, rank), jnp.float32)],
        compiler_params=pltpu.CompilerParams(vmem_limit_bytes=32 * 2**20),
        name="orthonormal_basis",
    )(p)


def core_kernel(modes, parts, ut_ref, f_ref, c_ref, local, send, recv, own_sem):
    me = lax.axis_index("mode")
    everyone = greet(modes, 1)
    width = f_ref.shape[1]
    cw = width // parts
    rows = c_ref.shape[0]
    sent = []
    for k in range(parts):
        local[:, pl.ds(k * cw, cw)] = dot(ut_ref[...], f_ref[:, pl.ds(k * cw, cw)], ((1,), (0,)))
        if k == 0:
            everyone()
        here = pl.ds(pl.multiple_of(me * width + k * cw, cw), cw)
        for d in range(modes - 1, 0, -1):
            peer = pairing(me, d, modes)
            copy = pltpu.make_async_remote_copy(
                src_ref=local.at[pl.ds(pl.multiple_of(peer * rows, rows), rows), pl.ds(k * cw, cw)],
                dst_ref=c_ref.at[:, here],
                send_sem=send.at[k * (modes - 1) + d - 1],
                recv_sem=recv.at[k * (modes - 1) + d - 1],
                device_id={"mode": peer}, device_id_type=MESH,
            )
            copy.start()
            sent.append(copy)
    own = pltpu.make_async_copy(
        local.at[pl.ds(pl.multiple_of(me * rows, rows), rows)],
        c_ref.at[:, pl.ds(pl.multiple_of(me * width, width), width)],
        own_sem,
    )
    own.start()
    own.wait()
    for copy in sent:
        copy.wait()


def core(modes, ut, f):
    whole, width = f.shape
    rank = ut.shape[0]
    parts = 4 if width % 512 == 0 else 1
    vmem = pl.BlockSpec(memory_space=pltpu.VMEM)
    dma = pltpu.SemaphoreType.DMA
    return pl.pallas_call(
        functools.partial(core_kernel, modes, parts),
        out_shape=jax.ShapeDtypeStruct((rank // modes, width * modes), jnp.float32),
        in_specs=[vmem, vmem],
        out_specs=vmem,
        scratch_shapes=[
            pltpu.VMEM((rank, width), jnp.float32),
            dma((parts * (modes - 1),)), dma((parts * (modes - 1),)),
            dma,
        ],
        compiler_params=pltpu.CompilerParams(
            collective_id=1, has_side_effects=True, vmem_limit_bytes=32 * 2**20
        ),
        name="core_tensor",
    )(ut, f)


def solution(mesh):
    modes, cols = mesh.shape["mode"], mesh.shape["cols"]

    def shards(snapshots, start_basis):
        fibres, projected = gather(modes, cols, snapshots, start_basis)
        subspace_basis, transposed = basis(projected)
        return subspace_basis, core(modes, transposed, fibres)

    return jax.shard_map(
        shards,
        mesh=mesh,
        in_specs=(P("mode", "cols"), P()),
        out_specs=(P(), P("mode", "cols")),
        check_vma=False,
    )
```

```python
import functools

import jax
import jax.numpy as jnp
from jax import lax
from jax.experimental import pallas as pl
from jax.experimental.pallas import tpu as pltpu
from jax.sharding import PartitionSpec as P

MESH = pl.DeviceIdType.MESH
SUB = 8


def dot(a, b, dims):
    return lax.dot_general(
        a,
        b,
        (dims, ((), ())),
        precision=lax.Precision.HIGHEST,
        preferred_element_type=jnp.float32,
    )


def pairing(me, d, modes):
    if modes & (modes - 1):
        return lax.rem(me + d, modes)
    peer = me
    bit = 1
    while bit < modes:
        if d & bit:
            peer = peer + bit * (1 - 2 * lax.rem(me // bit, 2))
        bit *= 2
    return peer


def small(a, b, dims):
    return lax.dot_general(a, b, (dims, ((), ())), preferred_element_type=jnp.float32)


def greet(modes, cols):
    me, mc = lax.axis_index("mode"), lax.axis_index("cols")
    barrier = pltpu.get_barrier_semaphore()
    for d in range(1, modes):
        pl.semaphore_signal(
            barrier, inc=1, device_id={"mode": lax.rem(me + d, modes)}, device_id_type=MESH
        )
    for d in range(1, cols):
        pl.semaphore_signal(
            barrier, inc=1, device_id={"cols": lax.rem(mc + d, cols)}, device_id_type=MESH
        )
    return lambda: pl.semaphore_wait(barrier, modes - 1 + cols - 1)


def gather_kernel(
    modes, cols, parts,
    x_ref, b_ref, f_ref, p_ref,
    basis, part, piece, slots_c, slots_m,
    own_sem, basis_sem, s0, r0, s1, r1, s2, r2, s3, r3, s4, r4,
):
    me, mc = lax.axis_index("mode"), lax.axis_index("cols")
    rows = x_ref.shape[0]
    width = f_ref.shape[1]
    cw = width // parts
    whole = f_ref.shape[0]

    def put(src, dst, send, recv, axis, peer):
        return pltpu.make_async_remote_copy(
            src_ref=src, dst_ref=dst, send_sem=send, recv_sem=recv,
            device_id={axis: peer}, device_id_type=MESH,
        )

    my_rows = pl.ds(pl.multiple_of(me * rows, rows), rows)
    everyone = greet(modes, cols)
    start = pltpu.make_async_copy(b_ref, basis, basis_sem)
    start.start()
    own = []
    for k in range(parts):
        copy = pltpu.make_async_copy(
            x_ref.at[:, pl.ds(pl.multiple_of(me * width + k * cw, cw), cw)],
            f_ref.at[my_rows, pl.ds(k * cw, cw)],
            own_sem.at[k],
        )
        copy.start()
        own.append(copy)

    everyone()

    sent = [[] for _ in range(parts)]

    def send(k, rounds):
        for d in rounds:
            peer = pairing(me, d, modes)
            copy = put(
                x_ref.at[:, pl.ds(pl.multiple_of(peer * width + k * cw, cw), cw)],
                f_ref.at[my_rows, pl.ds(k * cw, cw)],
                s0.at[k * (modes - 1) + d - 1], r0.at[k * (modes - 1) + d - 1], "mode", peer,
            )
            copy.start()
            sent[k].append(copy)

    far = range(modes - 1, modes // 2 - 1, -1)
    near = range(modes // 2 - 1, 0, -1)
    for k in range(parts):
        send(k, far)
        if k > 0:
            send(k - 1, near)
    send(parts - 1, near)

    start.wait()
    bt = basis[...].T
    for k in range(parts):
        own[k].wait()
        for copy in sent[k]:
            copy.wait_recv()
        fk = f_ref[:, pl.ds(k * cw, cw)]
        t = dot(bt, fk, ((1,), (0,)))
        term = dot(fk, t, ((1,), (1,)))
        if k == 0:
            part[...] = term
        else:
            part[...] += term

    rc = whole // cols
    mine = pl.ds(pl.multiple_of(mc * rc, rc), rc)
    first = []
    for d in range(1, cols):
        peer = lax.rem(mc + d, cols)
        copy = put(
            part.at[pl.ds(pl.multiple_of(peer * rc, rc), rc)],
            slots_c.at[d - 1], s1.at[d - 1], r1.at[d - 1], "cols", peer,
        )
        copy.start()
        first.append(copy)
    for copy in first:
        copy.wait_recv()
    total = part[mine, :]
    for d in range(1, cols):
        total = total + slots_c[d - 1]
    piece[...] = total

    sl = slots_m.shape[1]
    owners = rc // sl

    def guarded(flag, body):
        if owners == modes:
            body()
        else:
            pl.when(flag)(body)

    second = []
    for d in range(modes - 1, 0, -1):
        peer = pairing(me, d, modes)
        place = peer if owners == modes else lax.rem(peer, owners)
        copy = put(
            piece.at[pl.ds(pl.multiple_of(place * sl, sl), sl)],
            slots_m.at[d - 1], s2.at[d - 1], r2.at[d - 1], "mode", peer,
        )
        guarded(peer < owners, copy.start)
        second.append((copy, peer))
    for copy, _ in second:
        guarded(me < owners, copy.wait_recv)
    place = me if owners == modes else lax.rem(me, owners)
    target = pl.ds(pl.multiple_of(mc * rc + place * sl, sl), sl)

    def add():
        total = piece[pl.ds(pl.multiple_of(place * sl, sl), sl), :]
        for d in range(1, modes):
            total = total + slots_m[d - 1]
        p_ref[target, :] = total

    guarded(me < owners, add)

    third = []
    for d in range(modes - 1, 0, -1):
        peer = pairing(me, d, modes)
        copy = put(p_ref.at[target], p_ref.at[target], s3.at[d - 1], r3.at[d - 1], "mode", peer)
        guarded(me < owners, copy.start)
        third.append(copy)
    fourth = []

    def forward(d, source):
        spot = source if owners == modes else lax.rem(source, owners)
        rows_of = pl.ds(pl.multiple_of(mc * rc + spot * sl, sl), sl)
        for e in range(1, cols):
            at = d * (cols - 1) + e - 1
            copy = put(
                p_ref.at[rows_of], p_ref.at[rows_of], s4.at[at], r4.at[at],
                "cols", lax.rem(mc + e, cols),
            )
            guarded(source < owners, copy.start)
            fourth.append((copy, source))

    forward(0, me)
    for d in range(1, modes):
        source = pairing(me, d, modes) if modes & (modes - 1) == 0 else lax.rem(me + modes - d, modes)
        guarded(source < owners, third[modes - 1 - d].wait_recv)
        forward(d, source)
    for copy, source in fourth:
        guarded(source < owners, copy.wait_recv)

    for row in sent:
        for copy in row:
            copy.wait_send()
    for copy in first:
        copy.wait_send()
    for copy, peer in second:
        guarded(peer < owners, copy.wait_send)
    for copy in third:
        guarded(me < owners, copy.wait_send)
    for copy, source in fourth:
        guarded(source < owners, copy.wait_send)


def gather(modes, cols, x, b):
    rows, local = x.shape
    whole, width = rows * modes, local // modes
    rank = b.shape[1]
    parts = 4 if width % 512 == 0 else 1
    rc = whole // cols
    sl = max(SUB, rc // modes)
    dma = pltpu.SemaphoreType.DMA
    vmem = pl.BlockSpec(memory_space=pltpu.VMEM)
    return pl.pallas_call(
        functools.partial(gather_kernel, modes, cols, parts),
        out_shape=(
            jax.ShapeDtypeStruct((whole, width), jnp.float32),
            jax.ShapeDtypeStruct((whole, rank), jnp.float32),
        ),
        in_specs=[pl.BlockSpec(memory_space=pltpu.HBM)] * 2,
        out_specs=(vmem, vmem),
        scratch_shapes=[
            pltpu.VMEM((whole, rank), jnp.float32),
            pltpu.VMEM((whole, rank), jnp.float32),
            pltpu.VMEM((rc, rank), jnp.float32),
            pltpu.VMEM((cols - 1, rc, rank), jnp.float32),
            pltpu.VMEM((modes - 1, sl, rank), jnp.float32),
            dma((parts,)), dma,
            dma((parts * (modes - 1),)), dma((parts * (modes - 1),)),
            dma((cols - 1,)), dma((cols - 1,)),
            dma((modes - 1,)), dma((modes - 1,)),
            dma((modes - 1,)), dma((modes - 1,)),
            dma((modes * (cols - 1),)), dma((modes * (cols - 1),)),
        ],
        compiler_params=pltpu.CompilerParams(
            collective_id=0, has_side_effects=True, vmem_limit_bytes=32 * 2**20
        ),
        name="gather_project",
    )(x, b)


def tree(terms):
    while len(terms) > 1:
        terms = [sum(terms[i:i + 2][1:], terms[i]) for i in range(0, len(terms), 2)]
    return terms[0]


def inverse_factor(a, out_ref):
    n = a.shape[0]
    count = n // SUB
    shape = (SUB, n)
    row_id = lax.broadcasted_iota(jnp.int32, shape, 0)
    col_id = lax.broadcasted_iota(jnp.int32, shape, 1)
    blocks = [a[SUB * i:SUB * (i + 1), :] for i in range(count)]
    duals = [
        jnp.where(col_id == row_id + SUB * i, 1.0, 0.0).astype(jnp.float32) for i in range(count)
    ]

    def row(block, i):
        return jnp.broadcast_to(block[i:i + 1, :], shape)

    def column(block, j):
        return jnp.broadcast_to(block[:, j:j + 1], shape)

    for at in range(count):
        base = SUB * at
        diagonal = [column(blocks[at], base + k) for k in range(SUB)]
        block, dual, lower = blocks[at], duals[at], duals[at]
        for k in range(0, SUB, 2):
            c0, c1 = diagonal[k], diagonal[k + 1]
            p, q, r = row(c0, k), row(c1, k), row(c1, k + 1)
            idet = 1.0 / (p * r - q * q)
            i00, i01, i11 = r * idet, -q * idet, p * idet

            def solve(m):
                m0, m1 = row(m, k), row(m, k + 1)
                return i00 * m0 + i01 * m1, i01 * m0 + i11 * m1

            def step(m):
                x0, x1 = solve(m)
                rest = m - (c0 * x0 + c1 * x1)
                return jnp.where(row_id == k, x0, jnp.where(row_id == k + 1, x1, rest))

            for later in range(k + 2, SUB):
                diagonal[later] = step(diagonal[later])
            v0, v1 = row(lower, k), row(lower, k + 1)
            out_ref[base + k:base + k + 1, :] = (v0 * lax.rsqrt(p))[0:1, :]
            out_ref[base + k + 1:base + k + 2, :] = ((v1 - (q / p) * v0) * jnp.sqrt(i11))[0:1, :]
            if k + 2 < SUB:
                y0, y1 = solve(lower)
                lower = jnp.where(row_id > k + 1, lower - (c0 * y0 + c1 * y1), lower)
            block, dual = step(block), step(dual)
        if at + 1 == count:
            break
        xs = [row(block, k) for k in range(SUB)]
        ys = [row(dual, k) for k in range(SUB)]
        for i in range(at + 1, count):
            cs = [column(blocks[i], base + k) for k in range(SUB)]
            blocks[i] = blocks[i] - tree([c * x for c, x in zip(cs, xs)])
            duals[i] = duals[i] - tree([c * y for c, y in zip(cs, ys)])


def basis_kernel(p_ref, u_ref, ut_ref, inverse):
    rank = p_ref.shape[1]
    rows = lax.broadcasted_iota(jnp.int32, (rank, rank), 0)
    columns = lax.broadcasted_iota(jnp.int32, (rank, rank), 1)
    eye = jnp.where(rows == columns, 1.0, 0.0).astype(jnp.float32)
    half = jnp.where(rows > columns, 1.0, 0.5 * eye)

    p = p_ref[...]
    p = p * lax.rsqrt(jnp.sum(p * p, axis=0, keepdims=True))
    inverse_factor(dot(p, p, ((0,), (0,))), inverse)
    q = dot(p, inverse[...], ((1,), (1,)))

    a = dot(q, q, ((0,), (0,)))
    e = a - eye
    near = jnp.sum(e * e) < 1e-6

    @pl.when(near)
    def _():
        low = half * e
        m = small(low, e, ((1,), (0,)))
        e1 = small(low + m, low, ((1,), (1,))) - m - m.T
        low1 = half * e1
        step = low + low1 - small(low1, low, ((1,), (0,)))
        u_ref[...] = q - small(q, step, ((1,), (1,)))

    @pl.when(jnp.logical_not(near))
    def _():
        inverse_factor(a, inverse)
        u_ref[...] = dot(q, inverse[...], ((1,), (1,)))

    ut_ref[...] = u_ref[...].T


def basis(p):
    vmem = pl.BlockSpec(memory_space=pltpu.VMEM)
    rank = p.shape[1]
    return pl.pallas_call(
        basis_kernel,
        out_shape=(
            jax.ShapeDtypeStruct(p.shape, jnp.float32),
            jax.ShapeDtypeStruct((rank, p.shape[0]), jnp.float32),
        ),
        in_specs=[vmem],
        out_specs=(vmem, vmem),
        scratch_shapes=[pltpu.VMEM((rank, rank), jnp.float32)],
        compiler_params=pltpu.CompilerParams(vmem_limit_bytes=32 * 2**20),
        name="orthonormal_basis",
    )(p)


def core_kernel(modes, parts, ut_ref, f_ref, c_ref, local, send, recv, own_sem):
    me = lax.axis_index("mode")
    everyone = greet(modes, 1)
    width = f_ref.shape[1]
    cw = width // parts
    rows = c_ref.shape[0]
    sent = []
    far = range(modes - 1, modes // 2 - 1, -1)
    near = range(modes // 2 - 1, 0, -1)

    def deliver(k, rounds):
        here = pl.ds(pl.multiple_of(me * width + k * cw, cw), cw)
        for d in rounds:
            peer = pairing(me, d, modes)
            copy = pltpu.make_async_remote_copy(
                src_ref=local.at[pl.ds(pl.multiple_of(peer * rows, rows), rows), pl.ds(k * cw, cw)],
                dst_ref=c_ref.at[:, here],
                send_sem=send.at[k * (modes - 1) + d - 1],
                recv_sem=recv.at[k * (modes - 1) + d - 1],
                device_id={"mode": peer}, device_id_type=MESH,
            )
            copy.start()
            sent.append(copy)

    for k in range(parts):
        local[:, pl.ds(k * cw, cw)] = dot(ut_ref[...], f_ref[:, pl.ds(k * cw, cw)], ((1,), (0,)))
        if k == 0:
            everyone()
        deliver(k, far)
        if k > 0:
            deliver(k - 1, near)
    deliver(parts - 1, near)
    own = pltpu.make_async_copy(
        local.at[pl.ds(pl.multiple_of(me * rows, rows), rows)],
        c_ref.at[:, pl.ds(pl.multiple_of(me * width, width), width)],
        own_sem,
    )
    own.start()
    own.wait()
    for copy in sent:
        copy.wait()


def core(modes, ut, f):
    whole, width = f.shape
    rank = ut.shape[0]
    parts = 4 if width % 512 == 0 else 1
    vmem = pl.BlockSpec(memory_space=pltpu.VMEM)
    dma = pltpu.SemaphoreType.DMA
    return pl.pallas_call(
        functools.partial(core_kernel, modes, parts),
        out_shape=jax.ShapeDtypeStruct((rank // modes, width * modes), jnp.float32),
        in_specs=[vmem, vmem],
        out_specs=vmem,
        scratch_shapes=[
            pltpu.VMEM((rank, width), jnp.float32),
            dma((parts * (modes - 1),)), dma((parts * (modes - 1),)),
            dma,
        ],
        compiler_params=pltpu.CompilerParams(
            collective_id=1, has_side_effects=True, vmem_limit_bytes=32 * 2**20
        ),
        name="core_tensor",
    )(ut, f)


def solution(mesh):
    modes, cols = mesh.shape["mode"], mesh.shape["cols"]

    def shards(snapshots, start_basis):
        fibres, projected = gather(modes, cols, snapshots, start_basis)
        subspace_basis, transposed = basis(projected)
        return subspace_basis, core(modes, transposed, fibres)

    return jax.shard_map(
        shards,
        mesh=mesh,
        in_specs=(P("mode", "cols"), P()),
        out_specs=(P(), P("mode", "cols")),
        check_vma=False,
    )
```

```python
import functools

import jax
import jax.numpy as jnp
from jax import lax
from jax.experimental import pallas as pl
from jax.experimental.pallas import tpu as pltpu
from jax.sharding import PartitionSpec as P

MESH = pl.DeviceIdType.MESH
SUB = 8


def dot(a, b, dims):
    return lax.dot_general(
        a,
        b,
        (dims, ((), ())),
        precision=lax.Precision.HIGHEST,
        preferred_element_type=jnp.float32,
    )


def pairing(me, d, modes):
    if modes & (modes - 1):
        return lax.rem(me + d, modes)
    peer = me
    bit = 1
    while bit < modes:
        if d & bit:
            peer = peer + bit * (1 - 2 * lax.rem(me // bit, 2))
        bit *= 2
    return peer


def small(a, b, dims):
    return lax.dot_general(a, b, (dims, ((), ())), preferred_element_type=jnp.float32)


def greet(modes, cols):
    me, mc = lax.axis_index("mode"), lax.axis_index("cols")
    barrier = pltpu.get_barrier_semaphore()
    for d in range(1, modes):
        pl.semaphore_signal(
            barrier, inc=1, device_id={"mode": lax.rem(me + d, modes)}, device_id_type=MESH
        )
    for d in range(1, cols):
        pl.semaphore_signal(
            barrier, inc=1, device_id={"cols": lax.rem(mc + d, cols)}, device_id_type=MESH
        )
    return lambda: pl.semaphore_wait(barrier, modes - 1 + cols - 1)


def gather_kernel(
    modes, cols, parts,
    x_ref, b_ref, f_ref, p_ref,
    basis, part, piece, slots_c, slots_m,
    own_sem, basis_sem, s0, r0, s1, r1, s2, r2, s3, r3, s4, r4,
):
    me, mc = lax.axis_index("mode"), lax.axis_index("cols")
    rows = x_ref.shape[0]
    width = f_ref.shape[1]
    cw = width // parts
    whole = f_ref.shape[0]

    def put(src, dst, send, recv, axis, peer):
        return pltpu.make_async_remote_copy(
            src_ref=src, dst_ref=dst, send_sem=send, recv_sem=recv,
            device_id={axis: peer}, device_id_type=MESH,
        )

    my_rows = pl.ds(pl.multiple_of(me * rows, rows), rows)
    everyone = greet(modes, cols)
    start = pltpu.make_async_copy(b_ref, basis, basis_sem)
    start.start()
    own = []
    for k in range(parts):
        copy = pltpu.make_async_copy(
            x_ref.at[:, pl.ds(pl.multiple_of(me * width + k * cw, cw), cw)],
            f_ref.at[my_rows, pl.ds(k * cw, cw)],
            own_sem.at[k],
        )
        copy.start()
        own.append(copy)

    everyone()

    sent = [[] for _ in range(parts)]

    def send(k, rounds):
        for d in rounds:
            peer = pairing(me, d, modes)
            copy = put(
                x_ref.at[:, pl.ds(pl.multiple_of(peer * width + k * cw, cw), cw)],
                f_ref.at[my_rows, pl.ds(k * cw, cw)],
                s0.at[k * (modes - 1) + d - 1], r0.at[k * (modes - 1) + d - 1], "mode", peer,
            )
            copy.start()
            sent[k].append(copy)

    far = range(modes - 1, modes // 2 - 1, -1)
    near = range(modes // 2 - 1, 0, -1)
    for k in range(parts):
        send(k, far)
        if k > 0:
            send(k - 1, near)
    send(parts - 1, near)

    start.wait()
    bt = basis[...].T
    for k in range(parts):
        own[k].wait()
        for copy in sent[k]:
            copy.wait_recv()
        fk = f_ref[:, pl.ds(k * cw, cw)]
        t = dot(bt, fk, ((1,), (0,)))
        if k == parts - 1:
            break
        term = dot(fk, t, ((1,), (1,)))
        if k == 0:
            part[...] = term
        else:
            part[...] += term

    rc = whole // cols
    mine = pl.ds(pl.multiple_of(mc * rc, rc), rc)
    def last(rows_of):
        term = dot(f_ref[rows_of, pl.ds(width - cw, cw)], t, ((1,), (1,)))
        part[rows_of, :] = term if parts == 1 else part[rows_of, :] + term

    first = []
    for d in range(1, cols):
        peer = lax.rem(mc + d, cols)
        last(pl.ds(pl.multiple_of(peer * rc, rc), rc))
        copy = put(
            part.at[pl.ds(pl.multiple_of(peer * rc, rc), rc)],
            slots_c.at[d - 1], s1.at[d - 1], r1.at[d - 1], "cols", peer,
        )
        copy.start()
        first.append(copy)
    last(mine)
    for copy in first:
        copy.wait_recv()
    total = part[mine, :]
    for d in range(1, cols):
        total = total + slots_c[d - 1]
    piece[...] = total

    sl = slots_m.shape[1]
    owners = rc // sl

    def guarded(flag, body):
        if owners == modes:
            body()
        else:
            pl.when(flag)(body)

    second = []
    for d in range(modes - 1, 0, -1):
        peer = pairing(me, d, modes)
        place = peer if owners == modes else lax.rem(peer, owners)
        copy = put(
            piece.at[pl.ds(pl.multiple_of(place * sl, sl), sl)],
            slots_m.at[d - 1], s2.at[d - 1], r2.at[d - 1], "mode", peer,
        )
        guarded(peer < owners, copy.start)
        second.append((copy, peer))
    for copy, _ in second:
        guarded(me < owners, copy.wait_recv)
    place = me if owners == modes else lax.rem(me, owners)
    target = pl.ds(pl.multiple_of(mc * rc + place * sl, sl), sl)

    def add():
        total = piece[pl.ds(pl.multiple_of(place * sl, sl), sl), :]
        for d in range(1, modes):
            total = total + slots_m[d - 1]
        p_ref[target, :] = total

    guarded(me < owners, add)

    third = []
    for d in range(modes - 1, 0, -1):
        peer = pairing(me, d, modes)
        copy = put(p_ref.at[target], p_ref.at[target], s3.at[d - 1], r3.at[d - 1], "mode", peer)
        guarded(me < owners, copy.start)
        third.append(copy)
    fourth = []

    def forward(d, source):
        spot = source if owners == modes else lax.rem(source, owners)
        rows_of = pl.ds(pl.multiple_of(mc * rc + spot * sl, sl), sl)
        for e in range(1, cols):
            at = d * (cols - 1) + e - 1
            copy = put(
                p_ref.at[rows_of], p_ref.at[rows_of], s4.at[at], r4.at[at],
                "cols", lax.rem(mc + e, cols),
            )
            guarded(source < owners, copy.start)
            fourth.append((copy, source))

    forward(0, me)
    for d in range(1, modes):
        source = pairing(me, d, modes) if modes & (modes - 1) == 0 else lax.rem(me + modes - d, modes)
        guarded(source < owners, third[modes - 1 - d].wait_recv)
        forward(d, source)
    for copy, source in fourth:
        guarded(source < owners, copy.wait_recv)

    for row in sent:
        for copy in row:
            copy.wait_send()
    for copy in first:
        copy.wait_send()
    for copy, peer in second:
        guarded(peer < owners, copy.wait_send)
    for copy in third:
        guarded(me < owners, copy.wait_send)
    for copy, source in fourth:
        guarded(source < owners, copy.wait_send)


def gather(modes, cols, x, b):
    rows, local = x.shape
    whole, width = rows * modes, local // modes
    rank = b.shape[1]
    parts = 4 if width % 512 == 0 else 1
    rc = whole // cols
    sl = max(SUB, rc // modes)
    dma = pltpu.SemaphoreType.DMA
    vmem = pl.BlockSpec(memory_space=pltpu.VMEM)
    return pl.pallas_call(
        functools.partial(gather_kernel, modes, cols, parts),
        out_shape=(
            jax.ShapeDtypeStruct((whole, width), jnp.float32),
            jax.ShapeDtypeStruct((whole, rank), jnp.float32),
        ),
        in_specs=[pl.BlockSpec(memory_space=pltpu.HBM)] * 2,
        out_specs=(vmem, vmem),
        scratch_shapes=[
            pltpu.VMEM((whole, rank), jnp.float32),
            pltpu.VMEM((whole, rank), jnp.float32),
            pltpu.VMEM((rc, rank), jnp.float32),
            pltpu.VMEM((cols - 1, rc, rank), jnp.float32),
            pltpu.VMEM((modes - 1, sl, rank), jnp.float32),
            dma((parts,)), dma,
            dma((parts * (modes - 1),)), dma((parts * (modes - 1),)),
            dma((cols - 1,)), dma((cols - 1,)),
            dma((modes - 1,)), dma((modes - 1,)),
            dma((modes - 1,)), dma((modes - 1,)),
            dma((modes * (cols - 1),)), dma((modes * (cols - 1),)),
        ],
        compiler_params=pltpu.CompilerParams(
            collective_id=0, has_side_effects=True, vmem_limit_bytes=32 * 2**20
        ),
        name="gather_project",
    )(x, b)


def tree(terms):
    while len(terms) > 1:
        terms = [sum(terms[i:i + 2][1:], terms[i]) for i in range(0, len(terms), 2)]
    return terms[0]


def inverse_factor(a, out_ref):
    n = a.shape[0]
    count = n // SUB
    shape = (SUB, n)
    row_id = lax.broadcasted_iota(jnp.int32, shape, 0)
    col_id = lax.broadcasted_iota(jnp.int32, shape, 1)
    blocks = [a[SUB * i:SUB * (i + 1), :] for i in range(count)]
    duals = [
        jnp.where(col_id == row_id + SUB * i, 1.0, 0.0).astype(jnp.float32) for i in range(count)
    ]

    def row(block, i):
        return jnp.broadcast_to(block[i:i + 1, :], shape)

    def column(block, j):
        return jnp.broadcast_to(block[:, j:j + 1], shape)

    for at in range(count):
        base = SUB * at
        diagonal = [column(blocks[at], base + k) for k in range(SUB)]
        block, dual, lower = blocks[at], duals[at], duals[at]
        for k in range(0, SUB, 2):
            c0, c1 = diagonal[k], diagonal[k + 1]
            p, q, r = row(c0, k), row(c1, k), row(c1, k + 1)
            idet = 1.0 / (p * r - q * q)
            i00, i01, i11 = r * idet, -q * idet, p * idet

            def solve(m):
                m0, m1 = row(m, k), row(m, k + 1)
                return i00 * m0 + i01 * m1, i01 * m0 + i11 * m1

            def step(m):
                x0, x1 = solve(m)
                rest = m - (c0 * x0 + c1 * x1)
                return jnp.where(row_id == k, x0, jnp.where(row_id == k + 1, x1, rest))

            for later in range(k + 2, SUB):
                diagonal[later] = step(diagonal[later])
            v0, v1 = row(lower, k), row(lower, k + 1)
            out_ref[base + k:base + k + 1, :] = (v0 * lax.rsqrt(p))[0:1, :]
            out_ref[base + k + 1:base + k + 2, :] = ((v1 - (q / p) * v0) * jnp.sqrt(i11))[0:1, :]
            if k + 2 < SUB:
                y0, y1 = solve(lower)
                lower = jnp.where(row_id > k + 1, lower - (c0 * y0 + c1 * y1), lower)
            block, dual = step(block), step(dual)
        if at + 1 == count:
            break
        xs = [row(block, k) for k in range(SUB)]
        ys = [row(dual, k) for k in range(SUB)]
        for i in range(at + 1, count):
            cs = [column(blocks[i], base + k) for k in range(SUB)]
            blocks[i] = blocks[i] - tree([c * x for c, x in zip(cs, xs)])
            duals[i] = duals[i] - tree([c * y for c, y in zip(cs, ys)])


def basis_kernel(p_ref, u_ref, ut_ref, inverse):
    rank = p_ref.shape[1]
    rows = lax.broadcasted_iota(jnp.int32, (rank, rank), 0)
    columns = lax.broadcasted_iota(jnp.int32, (rank, rank), 1)
    eye = jnp.where(rows == columns, 1.0, 0.0).astype(jnp.float32)
    half = jnp.where(rows > columns, 1.0, 0.5 * eye)

    p = p_ref[...]
    p = p * lax.rsqrt(jnp.sum(p * p, axis=0, keepdims=True))
    inverse_factor(dot(p, p, ((0,), (0,))), inverse)
    q = dot(p, inverse[...], ((1,), (1,)))

    a = dot(q, q, ((0,), (0,)))
    e = a - eye
    near = jnp.sum(e * e) < 1e-6

    @pl.when(near)
    def _():
        low = half * e
        m = small(low, e, ((1,), (0,)))
        e1 = small(low + m, low, ((1,), (1,))) - m - m.T
        low1 = half * e1
        step = low + low1 - small(low1, low, ((1,), (0,)))
        u_ref[...] = q - small(q, step, ((1,), (1,)))

    @pl.when(jnp.logical_not(near))
    def _():
        inverse_factor(a, inverse)
        u_ref[...] = dot(q, inverse[...], ((1,), (1,)))

    ut_ref[...] = u_ref[...].T


def basis(p):
    vmem = pl.BlockSpec(memory_space=pltpu.VMEM)
    rank = p.shape[1]
    return pl.pallas_call(
        basis_kernel,
        out_shape=(
            jax.ShapeDtypeStruct(p.shape, jnp.float32),
            jax.ShapeDtypeStruct((rank, p.shape[0]), jnp.float32),
        ),
        in_specs=[vmem],
        out_specs=(vmem, vmem),
        scratch_shapes=[pltpu.VMEM((rank, rank), jnp.float32)],
        compiler_params=pltpu.CompilerParams(vmem_limit_bytes=32 * 2**20),
        name="orthonormal_basis",
    )(p)


def core_kernel(modes, parts, ut_ref, f_ref, c_ref, local, send, recv, own_sem):
    me = lax.axis_index("mode")
    everyone = greet(modes, 1)
    width = f_ref.shape[1]
    cw = width // parts
    rows = c_ref.shape[0]
    sent = []
    for k in range(parts):
        local[:, pl.ds(k * cw, cw)] = dot(ut_ref[...], f_ref[:, pl.ds(k * cw, cw)], ((1,), (0,)))
        if k == 0:
            everyone()
        here = pl.ds(pl.multiple_of(me * width + k * cw, cw), cw)
        for d in range(modes - 1, 0, -1):
            peer = pairing(me, d, modes)
            copy = pltpu.make_async_remote_copy(
                src_ref=local.at[pl.ds(pl.multiple_of(peer * rows, rows), rows), pl.ds(k * cw, cw)],
                dst_ref=c_ref.at[:, here],
                send_sem=send.at[k * (modes - 1) + d - 1],
                recv_sem=recv.at[k * (modes - 1) + d - 1],
                device_id={"mode": peer}, device_id_type=MESH,
            )
            copy.start()
            sent.append(copy)
    own = pltpu.make_async_copy(
        local.at[pl.ds(pl.multiple_of(me * rows, rows), rows)],
        c_ref.at[:, pl.ds(pl.multiple_of(me * width, width), width)],
        own_sem,
    )
    own.start()
    own.wait()
    for copy in sent:
        copy.wait()


def core(modes, ut, f):
    whole, width = f.shape
    rank = ut.shape[0]
    parts = 4 if width % 512 == 0 else 1
    vmem = pl.BlockSpec(memory_space=pltpu.VMEM)
    dma = pltpu.SemaphoreType.DMA
    return pl.pallas_call(
        functools.partial(core_kernel, modes, parts),
        out_shape=jax.ShapeDtypeStruct((rank // modes, width * modes), jnp.float32),
        in_specs=[vmem, vmem],
        out_specs=vmem,
        scratch_shapes=[
            pltpu.VMEM((rank, width), jnp.float32),
            dma((parts * (modes - 1),)), dma((parts * (modes - 1),)),
            dma,
        ],
        compiler_params=pltpu.CompilerParams(
            collective_id=1, has_side_effects=True, vmem_limit_bytes=32 * 2**20
        ),
        name="core_tensor",
    )(ut, f)


def solution(mesh):
    modes, cols = mesh.shape["mode"], mesh.shape["cols"]

    def shards(snapshots, start_basis):
        fibres, projected = gather(modes, cols, snapshots, start_basis)
        subspace_basis, transposed = basis(projected)
        return subspace_basis, core(modes, transposed, fibres)

    return jax.shard_map(
        shards,
        mesh=mesh,
        in_specs=(P("mode", "cols"), P()),
        out_specs=(P(), P("mode", "cols")),
        check_vma=False,
    )
```
